512 devices in a mesh: grp: 16 (over y, z_lo), dev: 32 (over x, z_hi, core).
Axes of the slice: x: 4, y: 8, z: 8 (z_hi: 4, z_lo: 2; z = z_hi * 2 + z_lo), core: 2. Of those that a mesh axis runs over, the one named last changes fastest.
Arguments:
- points: bfloat16 [1048576, 64], P(('grp', 'dev'))
- inv_scale: float32 [64], replicated, may hold values from 0.15 to 0.45
- probes: float32 [1048576, 32], P(('grp', 'dev'))
- noise: float32 [1], replicated, may hold values from 0.5 to 2
Outputs:
- normalized: float32 [1048576, 32], P(('grp', 'dev'))
- curvature: float32 [32], replicated
The draws below stay inside these ranges and needn't reach their ends.
All inputs are finite; a program needn't handle non-finite values.
Results may differ from the reference program's by a relative error of at most 0.0065.
Values may be sent and summed in bfloat16 or wider, within the bound.
No kernel may reach another device: no remote copies, remote signals or barrier semaphores. Data moves between devices by JAX's collectives and lax.ppermute only.
A program may use at most 64 MiB of HBM per device.

```python
import math
import jax
import jax.numpy as jnp
from jax import lax

BLOCK = 2048
FEATURES = 64
PROBES = 32
POINTS = 1048576
N_GRP = 16
N_DEV = 32


def draw_points(key, part):
    key = jax.random.fold_in(key, 1)
    key_base, key_scale = jax.random.split(key)
    base = jnp.clip(jax.random.normal(key_base, (POINTS, FEATURES), jnp.float32), -6.0, 6.0)
    scale = jnp.exp(jax.random.uniform(key_scale, (POINTS, 1), jnp.float32, math.log(0.3), math.log(1.2)))
    return (base * scale).astype(jnp.bfloat16)


def draw_probes(key, part):
    key = jax.random.fold_in(key, 2)
    key_base, key_rows, key_cols = jax.random.split(key, 3)
    position = jnp.arange(POINTS, dtype=jnp.float32)[:, None] / (POINTS - 1)
    row_scale = jnp.exp(jax.random.uniform(key_rows, (POINTS, 1), jnp.float32, math.log(0.3), math.log(3.0)))
    col_scale = jnp.exp(jax.random.uniform(key_cols, (1, PROBES), jnp.float32, math.log(0.3), math.log(3.0)))
    base = jnp.clip(jax.random.normal(key_base, (POINTS, PROBES), jnp.float32), -4.0, 4.0)
    rising = jnp.sqrt(1.0 + 2.0 * position)
    return (base * rising * row_scale * col_scale).astype(jnp.float32)


def setup_inputs(seed: int = 0) -> dict:
    key_list = jax.random.split(jax.random.key(seed), 5)
    return {
        "points": draw_points(jax.random.fold_in(key_list[4], 71), 0),
        "inv_scale": jnp.clip(jnp.exp(jax.random.uniform(key_list[1], (FEATURES,), jnp.float32, math.log(0.15), math.log(0.45))), 0.15, 0.45),
        "probes": draw_probes(jax.random.fold_in(key_list[4], 71), 0),
        "noise": jnp.clip(jnp.exp(jax.random.uniform(key_list[3], (1,), jnp.float32, math.log(0.5), math.log(2.0))), 0.5, 2.0),
    }


def matern(left, left_norm, right, right_norm):
    cross = lax.dot_general(left, right, (((1,), (1,)), ((), ())), preferred_element_type=jnp.float32)
    dist_sq = jnp.maximum(left_norm[:, None] + right_norm[None, :] - 2.0 * cross, 0.0)
    radius = 5.0 ** 0.5 * jnp.sqrt(dist_sq)
    return ((1.0 + radius + radius * radius / 3.0) * jnp.exp(-radius)).astype(jnp.bfloat16)

def reference(points, inv_scale, probes, noise):
    blocks = N_GRP * N_DEV
    scaled = (points.astype(jnp.float32) * inv_scale[None, :]).astype(jnp.bfloat16)
    norms = lax.optimization_barrier(jnp.sum(jnp.square(scaled.astype(jnp.float32)), axis=1))
    rounded = probes.astype(jnp.bfloat16)
    scaled_blocks = scaled.reshape(blocks, BLOCK, FEATURES)
    norm_blocks = norms.reshape(blocks, BLOCK)
    probe_blocks = rounded.reshape(blocks, BLOCK, PROBES)
    indices = jnp.arange(blocks, dtype=jnp.int32)

    def own_block(index):
        tile = matern(scaled_blocks[index], norm_blocks[index], scaled_blocks[index], norm_blocks[index])
        return jnp.dot(tile, probe_blocks[index], preferred_element_type=jnp.float32)
    product = noise[0] * probes.reshape(blocks, BLOCK, PROBES) + lax.map(own_block, indices)
    for offset in (1, N_DEV, N_DEV + 1):
        partners = ((indices - offset) % blocks).astype(jnp.int32)

        def pair_block(pair):
            index, partner = pair
            tile = matern(scaled_blocks[index], norm_blocks[index], scaled_blocks[partner], norm_blocks[partner])
            forward = jnp.dot(tile, probe_blocks[partner], preferred_element_type=jnp.float32)
            backward = lax.dot_general(tile, probe_blocks[index], (((0,), (0,)), ((), ())), preferred_element_type=jnp.float32)
            return (forward, backward)
        forward, backward = lax.map(pair_block, (indices, partners))
        product = product + forward + jnp.roll(backward, -offset, axis=0)
    product = product.reshape(POINTS, PROBES)
    wide_probes = rounded.astype(jnp.float32)
    curvature = lax.optimization_barrier(jnp.sum(wide_probes * product, axis=0)) / POINTS
    square = lax.optimization_barrier(jnp.sum(product * product, axis=0)) / POINTS
    normalized = product * lax.rsqrt(square + 1e-06)[None, :]
    return (normalized, curvature)
```

```python
import functools

import jax
import jax.numpy as jnp
from jax import lax
from jax.experimental import pallas as pl
from jax.experimental.pallas import tpu as pltpu
from jax.sharding import PartitionSpec as P

ROOT5 = 5.0**0.5
RATE = ROOT5 * 1.4426950408889634
DEPTH = 128
VMEM = pl.BlockSpec(memory_space=pltpu.VMEM)


def dot(left, right, dims):
    return lax.dot_general(left, right, (dims, ((), ())), preferred_element_type=jnp.float32)


def matern(dist_sq):
    dist_sq = jnp.maximum(dist_sq, 1e-30)
    dist = dist_sq * lax.rsqrt(dist_sq)
    decay = jnp.exp2(dist * -RATE)
    moved = dist + 1.5 / ROOT5
    return ((moved * moved + 0.15) * decay).astype(jnp.bfloat16)


def extended(features, left):
    wide = features.astype(jnp.float32)
    norms = jnp.sum(wide * wide, axis=0, keepdims=True)
    high = norms.astype(jnp.bfloat16).astype(jnp.float32)
    rest = norms - high
    mid = rest.astype(jnp.bfloat16).astype(jnp.float32)
    low = rest - mid
    first, ones = (3, 0) if left else (0, 3)
    row = lax.broadcasted_iota(jnp.int32, (DEPTH - features.shape[0], features.shape[1]), 0)
    extra = jnp.where((row >= ones) & (row < ones + 3), 1.0, 0.0)
    for k, part in enumerate((high, mid, low)):
        extra = jnp.where(row == first + k, part, extra)
    wide = wide * -2.0 if left else wide
    return jnp.concatenate([wide, extra], axis=0).astype(jnp.bfloat16)


def put_left(left_ref, features):
    left_ref[...] = extended(features, True).astype(jnp.float32).T.astype(jnp.bfloat16)


def fill(tile_ref, dist_ref):
    for row in range(0, dist_ref.shape[0], 32):
        tile_ref[row : row + 32, :] = matern(dist_ref[row : row + 32, :])


def pair_kernel(rows, cols, feats, own_ref, far_ref, out_ref, back_ref, left, right, dist0, dist1, tile0, tile1, back):
    count = own_ref.shape[1]
    per, steps = count // rows, (count // rows) * (count // cols)
    right[...] = extended(own_ref[:feats, :], False)
    put_left(left, far_ref[:feats, :])
    out_ref[...] = jnp.zeros_like(out_ref)
    back[...] = jnp.zeros_like(back)

    def spans(step):
        return (
            pl.ds(pl.multiple_of(lax.rem(step, per) * rows, rows), rows),
            pl.ds(pl.multiple_of(lax.div(step, per) * cols, cols), cols),
        )

    def measure(step, dist):
        far, own = spans(step)
        dist[...] = dot(left[far, :], right[:, own], ((1,), (0,)))

    def apply(step, tile):
        far, own = spans(step)
        out_ref[:, own] += dot(far_ref[feats:, far], tile[...], ((1,), (0,)))
        back[:, far] += dot(own_ref[feats:, own], tile[...], ((1,), (1,)))

    measure(jnp.int32(0), dist0)
    measure(jnp.int32(1), dist1)
    fill(tile0, dist0)

    def body(half, carry):
        step = 2 * half
        apply(step - 2, tile0)
        fill(tile1, dist1)
        measure(step, dist0)
        apply(step - 1, tile1)
        fill(tile0, dist0)
        measure(step + 1, dist1)
        return carry

    lax.fori_loop(1, steps // 2, body, 0)
    apply(jnp.int32(steps - 2), tile0)
    fill(tile1, dist1)
    apply(jnp.int32(steps - 1), tile1)
    back_ref[...] = back[...].astype(back_ref.dtype)


def pair(own, far, feats, rows=512, cols=256):
    count = own.shape[1]
    probes = own.shape[0] - feats
    return pl.pallas_call(
        functools.partial(pair_kernel, rows, cols, feats),
        out_shape=(
            jax.ShapeDtypeStruct((probes, count), jnp.float32),
            jax.ShapeDtypeStruct((probes, count), jnp.bfloat16),
        ),
        in_specs=[VMEM] * 2,
        out_specs=[VMEM] * 2,
        scratch_shapes=[
            pltpu.VMEM((count, DEPTH), jnp.bfloat16),
            pltpu.VMEM((DEPTH, count), jnp.bfloat16),
            pltpu.VMEM((rows, cols), jnp.float32),
            pltpu.VMEM((rows, cols), jnp.float32),
            pltpu.VMEM((rows, cols), jnp.bfloat16),
            pltpu.VMEM((rows, cols), jnp.bfloat16),
            pltpu.VMEM((probes, count), jnp.float32),
        ],
        compiler_params=pltpu.CompilerParams(vmem_limit_bytes=32 * 2**20),
        cost_estimate=pl.CostEstimate(
            flops=2 * count * count * (2 * 256 + DEPTH),
            bytes_accessed=count * 1000,
            transcendentals=2 * count * count,
        ),
    )(own, far)


def self_kernel(cols, feats, own_ref, out_ref, left, right, dist0, dist1, tile0, tile1):
    count = own_ref.shape[1]
    blocks = count // cols
    half = blocks // 2
    right[...] = extended(own_ref[:feats, :], False)
    put_left(left, own_ref[:feats, :])
    out_ref[...] = jnp.zeros_like(out_ref)

    def span(block):
        return pl.ds(pl.multiple_of(lax.rem(block, blocks) * cols, cols), cols)

    def measure(i, pieces, dist):
        for k, d in enumerate(pieces):
            dist[k * cols : (k + 1) * cols, :] = dot(left[span(i + d), :], right[:, span(i)], ((1,), (0,)))

    def apply(i, pieces, tile, both):
        total = jnp.zeros((out_ref.shape[0], cols), jnp.float32)
        for k, d in enumerate(pieces):
            part = tile[k * cols : (k + 1) * cols, :]
            total += dot(own_ref[feats:, span(i + d)], part, ((1,), (0,)))
            if both:
                out_ref[:, span(i + d)] += dot(own_ref[feats:, span(i)], part, ((1,), (1,)))
        out_ref[:, span(i)] += total

    once, twice = (0, half), tuple(range(1, half))
    measure(jnp.int32(0), once, dist0)
    measure(jnp.int32(0), twice, dist1)
    fill(tile0, dist0)

    def body(i, carry):
        apply(i - 1, once, tile0, False)
        fill(tile1, dist1)
        measure(i, once, dist0)
        apply(i - 1, twice, tile1, True)
        fill(tile0, dist0)
        measure(i, twice, dist1)
        return carry

    lax.fori_loop(1, blocks, body, 0)
    apply(jnp.int32(blocks - 1), once, tile0, False)
    fill(tile1, dist1)
    apply(jnp.int32(blocks - 1), twice, tile1, True)


def self_product(own, feats, cols=256):
    count = own.shape[1]
    probes = own.shape[0] - feats
    twice = (count // cols // 2 - 1) * cols
    return pl.pallas_call(
        functools.partial(self_kernel, cols, feats),
        out_shape=jax.ShapeDtypeStruct((probes, count), jnp.float32),
        in_specs=[VMEM],
        out_specs=VMEM,
        scratch_shapes=[
            pltpu.VMEM((count, DEPTH), jnp.bfloat16),
            pltpu.VMEM((DEPTH, count), jnp.bfloat16),
            pltpu.VMEM((2 * cols, cols), jnp.float32),
            pltpu.VMEM((twice, cols), jnp.float32),
            pltpu.VMEM((2 * cols, cols), jnp.bfloat16),
            pltpu.VMEM((twice, cols), jnp.bfloat16),
        ],
        compiler_params=pltpu.CompilerParams(vmem_limit_bytes=32 * 2**20),
        cost_estimate=pl.CostEstimate(
            flops=count * count * (3 * 256 + DEPTH),
            bytes_accessed=count * 500,
            transcendentals=count * count,
        ),
    )(own)


def from_behind(shard, by):
    count = lax.axis_size("grp") * lax.axis_size("dev")
    return lax.ppermute(shard, ("grp", "dev"), [(i, (i + by) % count) for i in range(count)])


def total(partial):
    for axis in ("dev", "grp"):
        size = lax.axis_size(axis)
        copies = jnp.broadcast_to(partial[None, :], (size, partial.shape[0]))
        partial = jnp.sum(lax.all_to_all(copies, axis, 0, 0), axis=0)
    return partial


def per_device(points, inv_scale, probes, noise):
    feats = points.shape[1]
    wide = probes.T
    scaled = (points.T.astype(jnp.float32) * inv_scale[:, None]).astype(jnp.bfloat16)
    rounded = wide.astype(jnp.bfloat16)
    own = jnp.concatenate([scaled, rounded], axis=0)
    width = lax.axis_size("dev")
    offsets = (1, width, width + 1)
    far = [from_behind(own, offset) for offset in offsets]
    parts = [self_product(own, feats)]
    for offset, other in zip(offsets, far):
        out, back = pair(own, other, feats)
        parts.append(out)
        parts.append(from_behind(back, -offset).astype(jnp.float32))
    product = noise[0] * wide + sum(parts) * (5.0 / 3.0)
    count = lax.axis_size("grp") * width * probes.shape[0]
    sums = total(
        jnp.concatenate([jnp.sum(rounded.astype(jnp.float32) * product, axis=1), jnp.sum(product * product, axis=1)])
    )
    mean = sums / count
    curvature, mean_square = jnp.split(mean, 2)
    normalized = product * lax.rsqrt(mean_square + 1e-06)[:, None]
    return (normalized.T, curvature)


def solution(mesh):
    placed = (P(("grp", "dev"), None), P(), P(("grp", "dev"), None), P())
    return jax.shard_map(
        per_device,
        mesh=mesh,
        in_specs=placed,
        out_specs=(P(("grp", "dev"), None), P()),
        check_vma=False,
    )
```

```python
import functools

import jax
import jax.numpy as jnp
from jax import lax
from jax.experimental import pallas as pl
from jax.experimental.pallas import tpu as pltpu
from jax.sharding import PartitionSpec as P

LOG2E = 1.4426950408889634
DEPTH = 256
EXTRA = 16
COLS = 256
ROWS = 512
VMEM = pl.BlockSpec(memory_space=pltpu.VMEM)
PARAMS = pltpu.CompilerParams(vmem_limit_bytes=32 * 2**20)


def dot(left, right, dims):
    return lax.dot_general(left, right, (dims, ((), ())), preferred_element_type=jnp.float32)


def matern(third_sq):
    third_sq = jnp.maximum(third_sq, 1e-30)
    third = third_sq * lax.rsqrt(third_sq)
    decay = jnp.exp2(third * (-3.0 * LOG2E))
    return ((third_sq + third + 1.0 / 3.0) * decay).astype(jnp.bfloat16)


def split3(wide):
    high = wide.astype(jnp.bfloat16)
    rest = wide - high.astype(jnp.float32)
    mid = rest.astype(jnp.bfloat16)
    low = (rest - mid.astype(jnp.float32)).astype(jnp.bfloat16)
    return high, mid, low


def extra_rows(features, left):
    wide = features.astype(jnp.float32)
    parts = split3(jnp.sum(wide * wide, axis=0, keepdims=True) * (5.0 / 9.0))
    row = lax.broadcasted_iota(jnp.int32, (EXTRA, features.shape[1]), 0)
    first, ones = (3, 0) if left else (0, 3)
    extra = jnp.where((row >= ones) & (row < ones + 3), 1.0, 0.0)
    for k, part in enumerate(parts):
        extra = jnp.where(row == first + k, part.astype(jnp.float32), extra)
    return extra.astype(jnp.bfloat16)


def left_side(features):
    feats, count = features.shape
    parts = split3(features.astype(jnp.float32) * (-10.0 / 9.0))
    rest = jnp.zeros((DEPTH - 3 * feats - EXTRA, count), jnp.bfloat16)
    return jnp.concatenate([*parts, extra_rows(features, True), rest], axis=0).T


def put_right(right, features):
    feats, count = features.shape
    for k in range(3):
        right[k * feats : (k + 1) * feats, :] = features
    right[3 * feats : 3 * feats + EXTRA, :] = extra_rows(features, False)
    right[3 * feats + EXTRA :, :] = jnp.zeros((DEPTH - 3 * feats - EXTRA, count), jnp.bfloat16)


def run_steps(steps, measure, apply, dists, tiles):
    def fill(step, slot):
        for row in range(0, step[1], 32):
            tiles[slot][row : row + 32, :] = matern(dists[slot][row : row + 32, :])

    count = len(steps)
    for k in range(count + 2):
        if k >= 2:
            apply(steps[k - 2], tiles[k % 2])
        if 1 <= k <= count:
            fill(steps[k - 1], (k - 1) % 2)
        if k < count:
            measure(steps[k], dists[k % 2])


def pair_kernel(feats, left_ref, own_ref, far_ref, acc_ref, out_ref, back_ref, right, dist0, dist1, tile0, tile1, back):
    count = own_ref.shape[1]
    put_right(right, far_ref[:feats, :])
    out_ref[...] = acc_ref[...]
    back[...] = jnp.zeros_like(back)

    def measure(step, dist):
        row, rows, col = step
        dist[...] = dot(left_ref[row : row + rows, :], right[:, col : col + COLS], ((1,), (0,)))

    def apply(step, tile):
        row, rows, col = step
        out_ref[:, row : row + rows] += dot(far_ref[feats:, col : col + COLS], tile[...], ((1,), (1,)))
        back[:, col : col + COLS] += dot(own_ref[feats:, row : row + rows], tile[...], ((1,), (0,)))

    steps = [(row, ROWS, col) for col in range(0, count, COLS) for row in range(0, count, ROWS)]
    run_steps(steps, measure, apply, (dist0, dist1), (tile0, tile1))
    back_ref[...] = back[...].astype(back_ref.dtype)


def stage_buffers():
    return [
        pltpu.VMEM((ROWS, COLS), jnp.float32),
        pltpu.VMEM((ROWS, COLS), jnp.float32),
        pltpu.VMEM((ROWS, COLS), jnp.bfloat16),
        pltpu.VMEM((ROWS, COLS), jnp.bfloat16),
    ]


def cost(elements):
    return pl.CostEstimate(flops=elements * 1500, bytes_accessed=2**20, transcendentals=2 * elements)


def pair(left, own, far, acc, feats):
    probes, count = acc.shape
    return pl.pallas_call(
        functools.partial(pair_kernel, feats),
        out_shape=(
            jax.ShapeDtypeStruct((probes, count), jnp.float32),
            jax.ShapeDtypeStruct((probes, count), jnp.bfloat16),
        ),
        in_specs=[VMEM] * 4,
        out_specs=[VMEM] * 2,
        scratch_shapes=[
            pltpu.VMEM((DEPTH, count), jnp.bfloat16),
            *stage_buffers(),
            pltpu.VMEM((probes, count), jnp.float32),
        ],
        compiler_params=PARAMS,
        cost_estimate=cost(count * count),
        name="pair_tile",
    )(left, own, far, acc)


def self_steps(cols):
    steps = []
    for col in cols:
        row = 0
        while row < col + COLS:
            rows = min(ROWS, col + COLS - row)
            steps.append((row, rows, col))
            row += rows
    return steps


def run_self(cols, feats, left_ref, own_ref, out_ref, right, dists, tiles):
    def measure(step, dist):
        row, rows, col = step
        dist[:rows, :] = dot(left_ref[row : row + rows, :], right[:, col : col + COLS], ((1,), (0,)))

    def apply(step, tile):
        row, rows, col = step
        above = min(rows, col - row)
        if above:
            out_ref[:, row : row + above] += dot(own_ref[feats:, col : col + COLS], tile[:above, :], ((1,), (1,)))
        out_ref[:, col : col + COLS] += dot(own_ref[feats:, row : row + rows], tile[:rows, :], ((1,), (0,)))

    run_steps(self_steps(cols), measure, apply, dists, tiles)


def first_kernel(cols, feats, own_ref, left_ref, out_ref, right, dist0, dist1, tile0, tile1):
    left_ref[...] = left_side(own_ref[:feats, :])
    put_right(right, own_ref[:feats, :])
    out_ref[...] = jnp.zeros_like(out_ref)
    run_self(cols, feats, left_ref, own_ref, out_ref, right, (dist0, dist1), (tile0, tile1))


def first_self(own, feats, cols):
    count = own.shape[1]
    probes = own.shape[0] - feats
    return pl.pallas_call(
        functools.partial(first_kernel, cols, feats),
        out_shape=(
            jax.ShapeDtypeStruct((count, DEPTH), jnp.bfloat16),
            jax.ShapeDtypeStruct((probes, count), jnp.float32),
        ),
        in_specs=[VMEM],
        out_specs=[VMEM] * 2,
        scratch_shapes=[pltpu.VMEM((DEPTH, count), jnp.bfloat16), *stage_buffers()],
        compiler_params=PARAMS,
        cost_estimate=cost(sum(step[1] for step in self_steps(cols)) * COLS),
        name="first_self",
    )(own)


def last_kernel(cols, feats, left_ref, own_ref, acc_ref, out_ref, right, dist0, dist1, tile0, tile1):
    put_right(right, own_ref[:feats, :])
    out_ref[...] = acc_ref[...]
    run_self(cols, feats, left_ref, own_ref, out_ref, right, (dist0, dist1), (tile0, tile1))


def last_self(left, own, acc, feats, cols):
    count = own.shape[1]
    return pl.pallas_call(
        functools.partial(last_kernel, cols, feats),
        out_shape=jax.ShapeDtypeStruct(acc.shape, jnp.float32),
        in_specs=[VMEM] * 3,
        out_specs=VMEM,
        scratch_shapes=[pltpu.VMEM((DEPTH, count), jnp.bfloat16), *stage_buffers()],
        compiler_params=PARAMS,
        cost_estimate=cost(sum(step[1] for step in self_steps(cols)) * COLS),
        name="last_self",
    )(left, own, acc)


def move(shard, by):
    count = lax.axis_size("grp") * lax.axis_size("dev")
    return lax.ppermute(shard, ("grp", "dev"), [(i, (i + by) % count) for i in range(count)])


def total(partial):
    for axis in ("dev", "grp"):
        size = lax.axis_size(axis)
        copies = jnp.broadcast_to(partial[None, :], (size, partial.shape[0]))
        partial = jnp.sum(lax.all_to_all(copies, axis, 0, 0), axis=0)
    return partial


def per_device(points, inv_scale, probes, noise):
    feats = points.shape[1]
    wide = probes.T
    scaled = (points.T.astype(jnp.float32) * inv_scale[:, None]).astype(jnp.bfloat16)
    rounded = wide.astype(jnp.bfloat16)
    own = jnp.concatenate([scaled, rounded], axis=0)
    width = lax.axis_size("dev")
    moves = (-1, width, width + 1)
    far = [move(own, by) for by in moves]
    columns = list(range(0, points.shape[0], COLS))
    late = len(columns) // 4
    left, acc = first_self(own, feats, columns[:-late])
    returned = jnp.zeros_like(wide)
    for by, other in zip(moves, far):
        acc, back = pair(left, own, other, acc, feats)
        returned = returned + move(back, -by).astype(jnp.float32)
    acc = last_self(left, own, acc, feats, columns[-late:])
    product = noise[0] * wide + (acc + returned) * 3.0
    count = lax.axis_size("grp") * width * probes.shape[0]
    sums = total(
        jnp.concatenate([jnp.sum(rounded.astype(jnp.float32) * product, axis=1), jnp.sum(product * product, axis=1)])
    )
    mean = sums / count
    curvature, mean_square = jnp.split(mean, 2)
    normalized = product * lax.rsqrt(mean_square + 1e-06)[:, None]
    return (normalized.T, curvature)


def solution(mesh):
    placed = (P(("grp", "dev"), None), P(), P(("grp", "dev"), None), P())
    return jax.shard_map(
        per_device,
        mesh=mesh,
        in_specs=placed,
        out_specs=(P(("grp", "dev"), None), P()),
        check_vma=False,
    )
```

```python
import functools

import jax
import jax.numpy as jnp
from jax import lax
from jax.experimental import pallas as pl
from jax.experimental.pallas import tpu as pltpu
from jax.sharding import PartitionSpec as P

LOG2E = 1.4426950408889634
DEPTH = 256
EXTRA = 16
COLS = 256
ROWS = 512
VMEM = pl.BlockSpec(memory_space=pltpu.VMEM)
COST = pl.CostEstimate(flops=1000, bytes_accessed=1000, transcendentals=0)
PARAMS = pltpu.CompilerParams(vmem_limit_bytes=32 * 2**20)


def dot(left, right, dims):
    return lax.dot_general(left, right, (dims, ((), ())), preferred_element_type=jnp.float32)


def matern(third_sq):
    third_sq = jnp.maximum(third_sq, 1e-30)
    third = third_sq * lax.rsqrt(third_sq)
    decay = jnp.exp2(third * (-3.0 * LOG2E))
    return ((third_sq + third + 1.0 / 3.0) * decay).astype(jnp.bfloat16)


def split3(wide):
    high = wide.astype(jnp.bfloat16)
    rest = wide - high.astype(jnp.float32)
    mid = rest.astype(jnp.bfloat16)
    low = (rest - mid.astype(jnp.float32)).astype(jnp.bfloat16)
    return high, mid, low


def extra_rows(features, left):
    wide = features.astype(jnp.float32)
    parts = split3(jnp.sum(wide * wide, axis=0, keepdims=True) * (5.0 / 9.0))
    row = lax.broadcasted_iota(jnp.int32, (EXTRA, features.shape[1]), 0)
    first, ones = (3, 0) if left else (0, 3)
    extra = jnp.where((row >= ones) & (row < ones + 3), 1.0, 0.0)
    for k, part in enumerate(parts):
        extra = jnp.where(row == first + k, part.astype(jnp.float32), extra)
    return extra.astype(jnp.bfloat16)


def left_side(features):
    feats, count = features.shape
    parts = split3(features.astype(jnp.float32) * (-10.0 / 9.0))
    rest = jnp.zeros((DEPTH - 3 * feats - EXTRA, count), jnp.bfloat16)
    return jnp.concatenate([*parts, extra_rows(features, True), rest], axis=0).T


def put_right(right, features):
    feats, count = features.shape
    for k in range(3):
        right[k * feats : (k + 1) * feats, :] = features
    right[3 * feats : 3 * feats + EXTRA, :] = extra_rows(features, False)
    right[3 * feats + EXTRA :, :] = jnp.zeros((DEPTH - 3 * feats - EXTRA, count), jnp.bfloat16)


def run_steps(steps, measure, apply, dists, tiles):
    def fill(step, slot):
        for row in range(0, step[1], 32):
            tiles[slot][row : row + 32, :] = matern(dists[slot][row : row + 32, :])

    count = len(steps)
    for k in range(count + 2):
        if k >= 2:
            apply(steps[k - 2], tiles[k % 2])
        if 1 <= k <= count:
            fill(steps[k - 1], (k - 1) % 2)
        if k < count:
            measure(steps[k], dists[k % 2])


def pair_kernel(feats, names, *refs):
    ref = dict(zip(names, refs))
    rows_ref, cols_ref, right, out, back = (ref[name] for name in ("rows", "cols", "right", "out", "back"))
    count = rows_ref.shape[1]
    left = ref["made"] if "made" in ref else ref["left"]
    if "made" in ref:
        left[...] = left_side(rows_ref[:feats, :])
    put_right(right, cols_ref[:feats, :])
    out[...] = ref["acc"][...]
    back[...] = ref["back_acc"][...] if "back_acc" in ref else jnp.zeros_like(back)

    def measure(step, dist):
        row, rows, col = step
        dist[...] = dot(left[row : row + rows, :], right[:, col : col + COLS], ((1,), (0,)))

    def apply(step, tile):
        row, rows, col = step
        out[:, row : row + rows] += dot(cols_ref[feats:, col : col + COLS], tile[...], ((1,), (1,)))
        back[:, col : col + COLS] += dot(rows_ref[feats:, row : row + rows], tile[...], ((1,), (0,)))

    steps = [(row, ROWS, col) for col in range(0, count, COLS) for row in range(0, count, ROWS)]
    run_steps(steps, measure, apply, (ref["dist0"], ref["dist1"]), (ref["tile0"], ref["tile1"]))
    ref["out_ref"][...] = out[...].astype(ref["out_ref"].dtype)
    ref["back_ref"][...] = back[...].astype(ref["back_ref"].dtype)


def stage_buffers():
    return [
        pltpu.VMEM((ROWS, COLS), jnp.float32),
        pltpu.VMEM((ROWS, COLS), jnp.float32),
        pltpu.VMEM((ROWS, COLS), jnp.bfloat16),
        pltpu.VMEM((ROWS, COLS), jnp.bfloat16),
    ]


def pair(rows, cols, acc, feats, left=None, back_acc=None, out_dtype=jnp.float32, back_dtype=jnp.float32):
    probes, count = acc.shape
    given = {"left": left, "rows": rows, "cols": cols, "acc": acc, "back_acc": back_acc}
    given = {name: value for name, value in given.items() if value is not None}
    made = {"right": pltpu.VMEM((DEPTH, count), jnp.bfloat16)}
    if left is None:
        made["made"] = pltpu.VMEM((count, DEPTH), jnp.bfloat16)
    made["out"] = made["back"] = pltpu.VMEM((probes, count), jnp.float32)
    names = [*given, "out_ref", "back_ref", *made, "dist0", "dist1", "tile0", "tile1"]
    return pl.pallas_call(
        functools.partial(pair_kernel, feats, names),
        out_shape=(
            jax.ShapeDtypeStruct((probes, count), out_dtype),
            jax.ShapeDtypeStruct((probes, count), back_dtype),
        ),
        in_specs=[VMEM] * len(given),
        out_specs=[VMEM] * 2,
        scratch_shapes=[*made.values(), *stage_buffers()],
        compiler_params=PARAMS,
        cost_estimate=COST,
        name="pair_tile",
    )(*given.values())


def self_steps(cols):
    steps = []
    for col in cols:
        row = 0
        while row < col + COLS:
            rows = min(ROWS, col + COLS - row)
            steps.append((row, rows, col))
            row += rows
    return steps


def run_self(cols, feats, left_ref, own_ref, out_ref, right, dists, tiles):
    def measure(step, dist):
        row, rows, col = step
        dist[:rows, :] = dot(left_ref[row : row + rows, :], right[:, col : col + COLS], ((1,), (0,)))

    def apply(step, tile):
        row, rows, col = step
        above = min(rows, col - row)
        if above:
            out_ref[:, row : row + above] += dot(own_ref[feats:, col : col + COLS], tile[:above, :], ((1,), (1,)))
        out_ref[:, col : col + COLS] += dot(own_ref[feats:, row : row + rows], tile[:rows, :], ((1,), (0,)))

    run_steps(self_steps(cols), measure, apply, dists, tiles)


def first_kernel(cols, feats, own_ref, left_ref, out_ref, right, dist0, dist1, tile0, tile1):
    left_ref[...] = left_side(own_ref[:feats, :])
    put_right(right, own_ref[:feats, :])
    out_ref[...] = jnp.zeros_like(out_ref)
    run_self(cols, feats, left_ref, own_ref, out_ref, right, (dist0, dist1), (tile0, tile1))


def first_self(own, feats, cols):
    count = own.shape[1]
    probes = own.shape[0] - feats
    return pl.pallas_call(
        functools.partial(first_kernel, cols, feats),
        out_shape=(
            jax.ShapeDtypeStruct((count, DEPTH), jnp.bfloat16),
            jax.ShapeDtypeStruct((probes, count), jnp.float32),
        ),
        in_specs=[VMEM],
        out_specs=[VMEM] * 2,
        scratch_shapes=[pltpu.VMEM((DEPTH, count), jnp.bfloat16), *stage_buffers()],
        compiler_params=PARAMS,
        cost_estimate=COST,
        name="first_self",
    )(own)


def last_kernel(cols, feats, left_ref, own_ref, acc_ref, more_ref, out_ref, right, dist0, dist1, tile0, tile1):
    put_right(right, own_ref[:feats, :])
    out_ref[...] = acc_ref[...] + more_ref[...].astype(jnp.float32)
    run_self(cols, feats, left_ref, own_ref, out_ref, right, (dist0, dist1), (tile0, tile1))


def last_self(left, own, acc, more, feats, cols):
    count = own.shape[1]
    return pl.pallas_call(
        functools.partial(last_kernel, cols, feats),
        out_shape=jax.ShapeDtypeStruct(acc.shape, jnp.float32),
        in_specs=[VMEM] * 4,
        out_specs=VMEM,
        scratch_shapes=[pltpu.VMEM((DEPTH, count), jnp.bfloat16), *stage_buffers()],
        compiler_params=PARAMS,
        cost_estimate=COST,
        name="last_self",
    )(left, own, acc, more)


def move(shard, by):
    count = lax.axis_size("grp") * lax.axis_size("dev")
    return lax.ppermute(shard, ("grp", "dev"), [(i, (i + by) % count) for i in range(count)])


def total(partial):
    for axis in ("dev", "grp"):
        size = lax.axis_size(axis)
        copies = jnp.broadcast_to(partial[None, :], (size, partial.shape[0]))
        partial = jnp.sum(lax.all_to_all(copies, axis, 0, 0), axis=0)
    return partial


def per_device(points, inv_scale, probes, noise):
    feats = points.shape[1]
    wide = probes.T
    scaled = (points.T.astype(jnp.float32) * inv_scale[:, None]).astype(jnp.bfloat16)
    rounded = wide.astype(jnp.bfloat16)
    own = jnp.concatenate([scaled, rounded], axis=0)
    width = lax.axis_size("dev")
    near = move(own, 1)
    wide_far = move(own, -width)
    columns = list(range(0, points.shape[0], COLS))
    late = len(columns) // 4
    left, acc = first_self(own, feats, columns[:-late])
    acc, near_acc = pair(own, near, acc, feats, left=left)
    to_near, far_acc = pair(near, wide_far, near_acc, feats, out_dtype=jnp.bfloat16)
    from_near = move(to_near, -1)
    acc, to_far = pair(own, wide_far, acc, feats, left=left, back_acc=far_acc, back_dtype=jnp.bfloat16)
    from_far = move(to_far, width)
    acc = last_self(left, own, acc, from_near, feats, columns[-late:])
    product = noise[0] * wide + (acc + from_far.astype(jnp.float32)) * 3.0
    count = lax.axis_size("grp") * width * probes.shape[0]
    sums = total(
        jnp.concatenate([jnp.sum(rounded.astype(jnp.float32) * product, axis=1), jnp.sum(product * product, axis=1)])
    )
    mean = sums / count
    curvature, mean_square = jnp.split(mean, 2)
    normalized = product * lax.rsqrt(mean_square + 1e-06)[:, None]
    return (normalized.T, curvature)


def solution(mesh):
    placed = (P(("grp", "dev"), None), P(), P(("grp", "dev"), None), P())
    return jax.shard_map(
        per_device,
        mesh=mesh,
        in_specs=placed,
        out_specs=(P(("grp", "dev"), None), P()),
        check_vma=False,
    )
```

```python
import functools

import jax
import jax.numpy as jnp
from jax import lax
from jax.experimental import pallas as pl
from jax.experimental.pallas import tpu as pltpu
from jax.sharding import PartitionSpec as P

LOG2E = 1.4426950408889634
DEPTH = 256
EXTRA = 16
COLS = 256
ROWS = 512
VMEM = pl.BlockSpec(memory_space=pltpu.VMEM)
COST = pl.CostEstimate(flops=1000, bytes_accessed=1000, transcendentals=0)
PARAMS = pltpu.CompilerParams(vmem_limit_bytes=32 * 2**20)


def dot(left, right, dims):
    return lax.dot_general(left, right, (dims, ((), ())), preferred_element_type=jnp.float32)


def matern(third_sq):
    third_sq = jnp.maximum(third_sq, 1e-30)
    third = third_sq * lax.rsqrt(third_sq)
    decay = jnp.exp2(third * (-3.0 * LOG2E))
    return ((third_sq + third + 1.0 / 3.0) * decay).astype(jnp.bfloat16)


def split3(wide):
    high = wide.astype(jnp.bfloat16)
    rest = wide - high.astype(jnp.float32)
    mid = rest.astype(jnp.bfloat16)
    low = (rest - mid.astype(jnp.float32)).astype(jnp.bfloat16)
    return high, mid, low


def extra_rows(features, left):
    wide = features.astype(jnp.float32)
    parts = split3(jnp.sum(wide * wide, axis=0, keepdims=True) * (5.0 / 9.0))
    row = lax.broadcasted_iota(jnp.int32, (EXTRA, features.shape[1]), 0)
    first, ones = (3, 0) if left else (0, 3)
    extra = jnp.where((row >= ones) & (row < ones + 3), 1.0, 0.0)
    for k, part in enumerate(parts):
        extra = jnp.where(row == first + k, part.astype(jnp.float32), extra)
    return extra.astype(jnp.bfloat16)


def left_side(features):
    feats, count = features.shape
    parts = split3(features.astype(jnp.float32) * (-10.0 / 9.0))
    rest = jnp.zeros((DEPTH - 3 * feats - EXTRA, count), jnp.bfloat16)
    return jnp.concatenate([*parts, extra_rows(features, True), rest], axis=0).T


def put_right(right, features):
    feats, count = features.shape
    for k in range(3):
        right[k * feats : (k + 1) * feats, :] = features
    right[3 * feats : 3 * feats + EXTRA, :] = extra_rows(features, False)
    right[3 * feats + EXTRA :, :] = jnp.zeros((DEPTH - 3 * feats - EXTRA, count), jnp.bfloat16)


def run_steps(steps, measure, apply, dists, tiles):
    def fill(step, slot):
        for row in range(0, step[1], 32):
            tiles[slot][row : row + 32, :] = matern(dists[slot][row : row + 32, :])

    count = len(steps)
    for k in range(count + 2):
        if k >= 2:
            apply(steps[k - 2], tiles[k % 2])
        if 1 <= k <= count:
            fill(steps[k - 1], (k - 1) % 2)
        if k < count:
            measure(steps[k], dists[k % 2])


def pair_kernel(feats, names, *refs):
    ref = dict(zip(names, refs))
    rows_ref, cols_ref, right, out, back = (ref[name] for name in ("rows", "cols", "right", "out", "back"))
    count = rows_ref.shape[1]
    left = ref["made"] if "made" in ref else ref["left"]
    if "made" in ref:
        left[...] = left_side(rows_ref[:feats, :])
    put_right(right, cols_ref[:feats, :])
    out[...] = ref["acc"][...]
    back[...] = ref["back_acc"][...] if "back_acc" in ref else jnp.zeros_like(back)

    def measure(step, dist):
        row, rows, col = step
        dist[...] = dot(left[row : row + rows, :], right[:, col : col + COLS], ((1,), (0,)))

    def apply(step, tile):
        row, rows, col = step
        out[:, row : row + rows] += dot(cols_ref[feats:, col : col + COLS], tile[...], ((1,), (1,)))
        back[:, col : col + COLS] += dot(rows_ref[feats:, row : row + rows], tile[...], ((1,), (0,)))

    steps = [(row, ROWS, col) for col in range(0, count, COLS) for row in range(0, count, ROWS)]
    run_steps(steps, measure, apply, (ref["dist0"], ref["dist1"]), (ref["tile0"], ref["tile1"]))
    ref["out_ref"][...] = out[...].astype(ref["out_ref"].dtype)
    ref["back_ref"][...] = back[...].astype(ref["back_ref"].dtype)


def stage_buffers():
    return [
        pltpu.VMEM((ROWS, COLS), jnp.float32),
        pltpu.VMEM((ROWS, COLS), jnp.float32),
        pltpu.VMEM((ROWS, COLS), jnp.bfloat16),
        pltpu.VMEM((ROWS, COLS), jnp.bfloat16),
    ]


def pair(rows, cols, acc, feats, left=None, back_acc=None, out_dtype=jnp.float32, back_dtype=jnp.float32):
    probes, count = acc.shape
    given = {"left": left, "rows": rows, "cols": cols, "acc": acc, "back_acc": back_acc}
    given = {name: value for name, value in given.items() if value is not None}
    made = {"right": pltpu.VMEM((DEPTH, count), jnp.bfloat16)}
    if left is None:
        made["made"] = pltpu.VMEM((count, DEPTH), jnp.bfloat16)
    made["out"] = made["back"] = pltpu.VMEM((probes, count), jnp.float32)
    names = [*given, "out_ref", "back_ref", *made, "dist0", "dist1", "tile0", "tile1"]
    return pl.pallas_call(
        functools.partial(pair_kernel, feats, names),
        out_shape=(
            jax.ShapeDtypeStruct((probes, count), out_dtype),
            jax.ShapeDtypeStruct((probes, count), back_dtype),
        ),
        in_specs=[VMEM] * len(given),
        out_specs=[VMEM] * 2,
        scratch_shapes=[*made.values(), *stage_buffers()],
        compiler_params=PARAMS,
        cost_estimate=COST,
        name="pair_tile",
    )(*given.values())


def self_steps(cols):
    steps = []
    for col in cols:
        row = 0
        while row < col + COLS:
            rows = min(ROWS, col + COLS - row)
            steps.append((row, rows, col))
            row += rows
    return steps


def run_self(cols, feats, left_ref, own_ref, out_ref, right, dists, tiles):
    def measure(step, dist):
        row, rows, col = step
        dist[:rows, :] = dot(left_ref[row : row + rows, :], right[:, col : col + COLS], ((1,), (0,)))

    def apply(step, tile):
        row, rows, col = step
        above = min(rows, col - row)
        if above:
            out_ref[:, row : row + above] += dot(own_ref[feats:, col : col + COLS], tile[:above, :], ((1,), (1,)))
        out_ref[:, col : col + COLS] += dot(own_ref[feats:, row : row + rows], tile[:rows, :], ((1,), (0,)))

    run_steps(self_steps(cols), measure, apply, dists, tiles)


def first_kernel(cols, feats, own_ref, left_ref, out_ref, copy_ref, right, dist0, dist1, tile0, tile1):
    left_ref[...] = left_side(own_ref[:feats, :])
    put_right(right, own_ref[:feats, :])
    out_ref[...] = jnp.zeros_like(out_ref)
    copy_ref[...] = own_ref[...]
    run_self(cols, feats, left_ref, own_ref, out_ref, right, (dist0, dist1), (tile0, tile1))


def first_self(own, feats, cols):
    count = own.shape[1]
    probes = own.shape[0] - feats
    return pl.pallas_call(
        functools.partial(first_kernel, cols, feats),
        out_shape=(
            jax.ShapeDtypeStruct((count, DEPTH), jnp.bfloat16),
            jax.ShapeDtypeStruct((probes, count), jnp.float32),
            jax.ShapeDtypeStruct(own.shape, own.dtype),
        ),
        in_specs=[VMEM],
        out_specs=[VMEM] * 3,
        scratch_shapes=[pltpu.VMEM((DEPTH, count), jnp.bfloat16), *stage_buffers()],
        compiler_params=PARAMS,
        cost_estimate=COST,
        name="first_self",
    )(own)


def last_kernel(cols, feats, left_ref, own_ref, acc_ref, more_ref, out_ref, right, dist0, dist1, tile0, tile1):
    put_right(right, own_ref[:feats, :])
    out_ref[...] = acc_ref[...] + more_ref[...].astype(jnp.float32)
    run_self(cols, feats, left_ref, own_ref, out_ref, right, (dist0, dist1), (tile0, tile1))


def last_self(left, own, acc, more, feats, cols):
    count = own.shape[1]
    return pl.pallas_call(
        functools.partial(last_kernel, cols, feats),
        out_shape=jax.ShapeDtypeStruct(acc.shape, jnp.float32),
        in_specs=[VMEM] * 4,
        out_specs=VMEM,
        scratch_shapes=[pltpu.VMEM((DEPTH, count), jnp.bfloat16), *stage_buffers()],
        compiler_params=PARAMS,
        cost_estimate=COST,
        name="last_self",
    )(left, own, acc, more)


def after_kernel(first_ref, own_ref, copy_ref):
    copy_ref[...] = own_ref[...]


def after(first, own):
    return pl.pallas_call(
        after_kernel,
        out_shape=jax.ShapeDtypeStruct(own.shape, own.dtype),
        in_specs=[VMEM] * 2,
        out_specs=VMEM,
        compiler_params=PARAMS,
        cost_estimate=COST,
        name="after",
    )(first, own)


def move(shard, by):
    count = lax.axis_size("grp") * lax.axis_size("dev")
    return lax.ppermute(shard, ("grp", "dev"), [(i, (i + by) % count) for i in range(count)])


def total(partial):
    for axis in ("dev", "grp"):
        size = lax.axis_size(axis)
        copies = jnp.broadcast_to(partial[None, :], (size, partial.shape[0]))
        partial = jnp.sum(lax.all_to_all(copies, axis, 0, 0), axis=0)
    return partial


def per_device(points, inv_scale, probes, noise):
    feats = points.shape[1]
    wide = probes.T
    scaled = (points.T.astype(jnp.float32) * inv_scale[:, None]).astype(jnp.bfloat16)
    rounded = wide.astype(jnp.bfloat16)
    own = jnp.concatenate([scaled, rounded], axis=0)
    width = lax.axis_size("dev")
    near = move(own, 1)
    columns = list(range(0, points.shape[0], COLS))
    late = len(columns) // 4
    left, acc, again = first_self(own, feats, columns[:-late])
    wide_far = move(after(near, again), -width)
    acc, near_acc = pair(own, near, acc, feats, left=left)
    to_near, far_acc = pair(near, wide_far, near_acc, feats, out_dtype=jnp.bfloat16)
    from_near = move(to_near, -1)
    acc, to_far = pair(own, wide_far, acc, feats, left=left, back_acc=far_acc, back_dtype=jnp.bfloat16)
    from_far = move(to_far, width)
    acc = last_self(left, own, acc, from_near, feats, columns[-late:])
    product = noise[0] * wide + (acc + from_far.astype(jnp.float32)) * 3.0
    count = lax.axis_size("grp") * width * probes.shape[0]
    sums = total(
        jnp.concatenate([jnp.sum(rounded.astype(jnp.float32) * product, axis=1), jnp.sum(product * product, axis=1)])
    )
    mean = sums / count
    curvature, mean_square = jnp.split(mean, 2)
    normalized = product * lax.rsqrt(mean_square + 1e-06)[:, None]
    return (normalized.T, curvature)


def solution(mesh):
    placed = (P(("grp", "dev"), None), P(), P(("grp", "dev"), None), P())
    return jax.shard_map(
        per_device,
        mesh=mesh,
        in_specs=placed,
        out_specs=(P(("grp", "dev"), None), P()),
        check_vma=False,
    )
```

```python
import functools

import jax
import jax.numpy as jnp
from jax import lax
from jax.experimental import pallas as pl
from jax.experimental.pallas import tpu as pltpu
from jax.sharding import PartitionSpec as P

LOG2E = 1.4426950408889634
DEPTH = 256
EXTRA = 16
COLS = 256
ROWS = 512
VMEM = pl.BlockSpec(memory_space=pltpu.VMEM)
COST = pl.CostEstimate(flops=1000, bytes_accessed=1000, transcendentals=0)
PARAMS = pltpu.CompilerParams(vmem_limit_bytes=32 * 2**20)


def dot(left, right, dims):
    return lax.dot_general(left, right, (dims, ((), ())), preferred_element_type=jnp.float32)


def matern(third_sq):
    third_sq = jnp.maximum(third_sq, 1e-30)
    third = third_sq * lax.rsqrt(third_sq)
    decay = jnp.exp2(third * (-3.0 * LOG2E))
    return ((third_sq + third + 1.0 / 3.0) * decay).astype(jnp.bfloat16)


def split3(wide):
    high = wide.astype(jnp.bfloat16)
    rest = wide - high.astype(jnp.float32)
    mid = rest.astype(jnp.bfloat16)
    low = (rest - mid.astype(jnp.float32)).astype(jnp.bfloat16)
    return high, mid, low


def extra_rows(features, left):
    wide = features.astype(jnp.float32)
    parts = split3(jnp.sum(wide * wide, axis=0, keepdims=True) * (5.0 / 9.0))
    row = lax.broadcasted_iota(jnp.int32, (EXTRA, features.shape[1]), 0)
    first, ones = (3, 0) if left else (0, 3)
    extra = jnp.where((row >= ones) & (row < ones + 3), 1.0, 0.0)
    for k, part in enumerate(parts):
        extra = jnp.where(row == first + k, part.astype(jnp.float32), extra)
    return extra.astype(jnp.bfloat16)


def left_side(features):
    feats, count = features.shape
    parts = split3(features.astype(jnp.float32) * (-10.0 / 9.0))
    rest = jnp.zeros((DEPTH - 3 * feats - EXTRA, count), jnp.bfloat16)
    return jnp.concatenate([*parts, extra_rows(features, True), rest], axis=0).T


def put_right(right, features):
    feats, count = features.shape
    for k in range(3):
        right[k * feats : (k + 1) * feats, :] = features
    right[3 * feats : 3 * feats + EXTRA, :] = extra_rows(features, False)
    right[3 * feats + EXTRA :, :] = jnp.zeros((DEPTH - 3 * feats - EXTRA, count), jnp.bfloat16)


def run_steps(steps, measure, apply, dists, tiles):
    def fill(step, slot):
        for row in range(0, step[1], 32):
            tiles[slot][row : row + 32, :] = matern(dists[slot][row : row + 32, :])

    count = len(steps)
    for k in range(count + 2):
        if k >= 2:
            apply(steps[k - 2], tiles[k % 2])
        if 1 <= k <= count:
            fill(steps[k - 1], (k - 1) % 2)
        if k < count:
            measure(steps[k], dists[k % 2])


def pair_kernel(feats, names, *refs):
    ref = dict(zip(names, refs))
    rows_ref, cols_ref, right, out, back = (ref[name] for name in ("rows", "cols", "right", "out", "back"))
    count = rows_ref.shape[1]
    left = ref["left"]
    if "next_left" in ref:
        ref["next_left"][...] = left_side(cols_ref[:feats, :])
    put_right(right, cols_ref[:feats, :])
    out[...] = ref["acc"][...]
    back[...] = ref["back_acc"][...] if "back_acc" in ref else jnp.zeros_like(back)

    def measure(step, dist):
        row, rows, col = step
        dist[...] = dot(left[row : row + rows, :], right[:, col : col + COLS], ((1,), (0,)))

    def apply(step, tile):
        row, rows, col = step
        out[:, row : row + rows] += dot(cols_ref[feats:, col : col + COLS], tile[...], ((1,), (1,)))
        back[:, col : col + COLS] += dot(rows_ref[feats:, row : row + rows], tile[...], ((1,), (0,)))

    steps = [(row, ROWS, col) for col in range(0, count, COLS) for row in range(0, count, ROWS)]
    run_steps(steps, measure, apply, (ref["dist0"], ref["dist1"]), (ref["tile0"], ref["tile1"]))
    ref["out_ref"][...] = out[...].astype(ref["out_ref"].dtype)
    ref["back_ref"][...] = back[...].astype(ref["back_ref"].dtype)


def stage_buffers():
    return [
        pltpu.VMEM((ROWS, COLS), jnp.float32),
        pltpu.VMEM((ROWS, COLS), jnp.float32),
        pltpu.VMEM((ROWS, COLS), jnp.bfloat16),
        pltpu.VMEM((ROWS, COLS), jnp.bfloat16),
    ]


def pair(left, rows, cols, acc, feats, back_acc=None, out_dtype=jnp.float32, back_dtype=jnp.float32, next_left=False):
    probes, count = acc.shape
    given = {"left": left, "rows": rows, "cols": cols, "acc": acc}
    if back_acc is not None:
        given["back_acc"] = back_acc
    results = {
        "out_ref": jax.ShapeDtypeStruct((probes, count), out_dtype),
        "back_ref": jax.ShapeDtypeStruct((probes, count), back_dtype),
    }
    if next_left:
        results["next_left"] = jax.ShapeDtypeStruct(left.shape, left.dtype)
    made = {
        "right": pltpu.VMEM((DEPTH, count), jnp.bfloat16),
        "out": pltpu.VMEM((probes, count), jnp.float32),
        "back": pltpu.VMEM((probes, count), jnp.float32),
    }
    names = [*given, *results, *made, "dist0", "dist1", "tile0", "tile1"]
    return pl.pallas_call(
        functools.partial(pair_kernel, feats, names),
        out_shape=tuple(results.values()),
        in_specs=[VMEM] * len(given),
        out_specs=(VMEM,) * len(results),
        scratch_shapes=[*made.values(), *stage_buffers()],
        compiler_params=PARAMS,
        cost_estimate=COST,
        name="pair_tile",
    )(*given.values())


def self_steps(cols):
    steps = []
    for col in cols:
        row = 0
        while row < col + COLS:
            rows = min(ROWS, col + COLS - row)
            steps.append((row, rows, col))
            row += rows
    return steps


def run_self(cols, feats, left_ref, own_ref, out_ref, right, dists, tiles):
    def measure(step, dist):
        row, rows, col = step
        dist[:rows, :] = dot(left_ref[row : row + rows, :], right[:, col : col + COLS], ((1,), (0,)))

    def apply(step, tile):
        row, rows, col = step
        above = min(rows, col - row)
        if above:
            out_ref[:, row : row + above] += dot(own_ref[feats:, col : col + COLS], tile[:above, :], ((1,), (1,)))
        out_ref[:, col : col + COLS] += dot(own_ref[feats:, row : row + rows], tile[:rows, :], ((1,), (0,)))

    run_steps(self_steps(cols), measure, apply, dists, tiles)


def first_kernel(cols, feats, noise_ref, wide_ref, own_ref, left_ref, out_ref, copy_ref, right, dist0, dist1, tile0, tile1):
    left_ref[...] = left_side(own_ref[:feats, :])
    put_right(right, own_ref[:feats, :])
    out_ref[...] = wide_ref[...] * (noise_ref[0] * (1.0 / 3.0))
    copy_ref[...] = own_ref[...]
    run_self(cols, feats, left_ref, own_ref, out_ref, right, (dist0, dist1), (tile0, tile1))


def first_self(noise, wide, own, feats, cols):
    count = own.shape[1]
    probes = own.shape[0] - feats
    return pl.pallas_call(
        functools.partial(first_kernel, cols, feats),
        out_shape=(
            jax.ShapeDtypeStruct((count, DEPTH), jnp.bfloat16),
            jax.ShapeDtypeStruct((probes, count), jnp.float32),
            jax.ShapeDtypeStruct(own.shape, own.dtype),
        ),
        in_specs=[pl.BlockSpec(memory_space=pltpu.SMEM), VMEM, VMEM],
        out_specs=[VMEM] * 3,
        scratch_shapes=[pltpu.VMEM((DEPTH, count), jnp.bfloat16), *stage_buffers()],
        compiler_params=PARAMS,
        cost_estimate=COST,
        name="first_self",
    )(noise, wide, own)


def last_kernel(cols, feats, left_ref, own_ref, acc_ref, more_ref, out_ref, right, dist0, dist1, tile0, tile1):
    put_right(right, own_ref[:feats, :])
    out_ref[...] = acc_ref[...] + more_ref[...].astype(jnp.float32)
    run_self(cols, feats, left_ref, own_ref, out_ref, right, (dist0, dist1), (tile0, tile1))


def last_self(left, own, acc, more, feats, cols):
    count = own.shape[1]
    return pl.pallas_call(
        functools.partial(last_kernel, cols, feats),
        out_shape=jax.ShapeDtypeStruct(acc.shape, jnp.float32),
        in_specs=[VMEM] * 4,
        out_specs=VMEM,
        scratch_shapes=[pltpu.VMEM((DEPTH, count), jnp.bfloat16), *stage_buffers()],
        compiler_params=PARAMS,
        cost_estimate=COST,
        name="last_self",
    )(left, own, acc, more)


def after_kernel(first_ref, own_ref, copy_ref):
    copy_ref[...] = own_ref[...]


def after(first, own):
    return pl.pallas_call(
        after_kernel,
        out_shape=jax.ShapeDtypeStruct(own.shape, own.dtype),
        in_specs=[VMEM] * 2,
        out_specs=VMEM,
        compiler_params=PARAMS,
        cost_estimate=COST,
        name="after",
    )(first, own)


def move(shard, by):
    count = lax.axis_size("grp") * lax.axis_size("dev")
    return lax.ppermute(shard, ("grp", "dev"), [(i, (i + by) % count) for i in range(count)])


def gather(partial, axis):
    size = lax.axis_size(axis)
    return lax.all_to_all(jnp.broadcast_to(partial[None, :], (size, partial.shape[0])), axis, 0, 0)


def finish_kernel(count, parts_ref, product_ref, out_ref, curvature_ref):
    probes = product_ref.shape[0]
    mean = jnp.sum(parts_ref[...], axis=0, keepdims=True) * (1.0 / count)
    curvature_ref[...] = mean[:, :probes]
    scale = lax.rsqrt(mean[:, probes:] + 1e-06)
    row = lax.broadcasted_iota(jnp.int32, (probes, probes), 0)
    col = lax.broadcasted_iota(jnp.int32, (probes, probes), 1)
    scale = jnp.sum(jnp.where(row == col, scale, 0.0), axis=1, keepdims=True)
    out_ref[...] = product_ref[...] * scale


def finish(parts, product, count):
    return pl.pallas_call(
        functools.partial(finish_kernel, count),
        out_shape=(
            jax.ShapeDtypeStruct(product.shape, jnp.float32),
            jax.ShapeDtypeStruct((1, product.shape[0]), jnp.float32),
        ),
        compiler_params=PARAMS,
        cost_estimate=COST,
        name="finish",
    )(parts, product)


def per_device(points, inv_scale, probes, noise):
    feats = points.shape[1]
    wide = probes.T
    scaled = (points.T.astype(jnp.float32) * inv_scale[:, None]).astype(jnp.bfloat16)
    rounded = wide.astype(jnp.bfloat16)
    own = jnp.concatenate([scaled, rounded], axis=0)
    width = lax.axis_size("dev")
    near = move(own, 1)
    columns = list(range(0, points.shape[0], COLS))
    late = len(columns) // 4
    left, acc, again = first_self(noise, wide, own, feats, columns[:-late])
    wide_far = move(after(near, again), -width)
    acc, near_acc, near_left = pair(left, own, near, acc, feats, next_left=True)
    to_near, far_acc = pair(near_left, near, wide_far, near_acc, feats, out_dtype=jnp.bfloat16)
    from_near = move(to_near, -1)
    acc, to_far = pair(left, own, wide_far, acc, feats, back_acc=far_acc, back_dtype=jnp.bfloat16)
    from_far = move(to_far, width)
    acc = last_self(left, own, acc, from_near, feats, columns[-late:])
    product = (acc + from_far.astype(jnp.float32)) * 3.0
    count = lax.axis_size("grp") * width * probes.shape[0]
    sums = jnp.concatenate(
        [jnp.sum(rounded.astype(jnp.float32) * product, axis=1), jnp.sum(product * product, axis=1)]
    )
    sums = jnp.sum(gather(sums, "dev"), axis=0)
    normalized, curvature = finish(gather(sums, "grp"), product, count)
    return (normalized.T, curvature[0])


def solution(mesh):
    placed = (P(("grp", "dev"), None), P(), P(("grp", "dev"), None), P())
    return jax.shard_map(
        per_device,
        mesh=mesh,
        in_specs=placed,
        out_specs=(P(("grp", "dev"), None), P()),
        check_vma=False,
    )
```

```python
import functools

import jax
import jax.numpy as jnp
from jax import lax
from jax.experimental import pallas as pl
from jax.experimental.pallas import tpu as pltpu
from jax.sharding import PartitionSpec as P

LOG2E = 1.4426950408889634
DEPTH = 256
EXTRA = 16
COLS = 256
ROWS = 512
VMEM = pl.BlockSpec(memory_space=pltpu.VMEM)
COST = pl.CostEstimate(flops=1000, bytes_accessed=1000, transcendentals=0)
PARAMS = pltpu.CompilerParams(vmem_limit_bytes=32 * 2**20)


def dot(left, right, dims):
    return lax.dot_general(left, right, (dims, ((), ())), preferred_element_type=jnp.float32)


def matern(third_sq):
    third_sq = jnp.maximum(third_sq, 1e-30)
    third = third_sq * lax.rsqrt(third_sq)
    decay = jnp.exp2(third * (-3.0 * LOG2E))
    return ((third_sq + (third + 1.0 / 3.0)) * decay).astype(jnp.bfloat16)


def split3(wide):
    high = wide.astype(jnp.bfloat16)
    rest = wide - high.astype(jnp.float32)
    mid = rest.astype(jnp.bfloat16)
    low = (rest - mid.astype(jnp.float32)).astype(jnp.bfloat16)
    return high, mid, low


def extra_rows(features, left):
    wide = features.astype(jnp.float32)
    parts = split3(jnp.sum(wide * wide, axis=0, keepdims=True) * (5.0 / 9.0))
    row = lax.broadcasted_iota(jnp.int32, (EXTRA, features.shape[1]), 0)
    first, ones = (3, 0) if left else (0, 3)
    extra = jnp.where((row >= ones) & (row < ones + 3), 1.0, 0.0)
    for k, part in enumerate(parts):
        extra = jnp.where(row == first + k, part.astype(jnp.float32), extra)
    return extra.astype(jnp.bfloat16)


def left_side(features):
    feats, count = features.shape
    parts = split3(features.astype(jnp.float32) * (-10.0 / 9.0))
    rest = jnp.zeros((DEPTH - 3 * feats - EXTRA, count), jnp.bfloat16)
    return jnp.concatenate([*parts, extra_rows(features, True), rest], axis=0).T


def put_right(right, features):
    feats, count = features.shape
    for k in range(3):
        right[k * feats : (k + 1) * feats, :] = features
    right[3 * feats : 3 * feats + EXTRA, :] = extra_rows(features, False)
    right[3 * feats + EXTRA :, :] = jnp.zeros((DEPTH - 3 * feats - EXTRA, count), jnp.bfloat16)


def run_steps(steps, measure, apply, dists, tiles):
    def fill(step, slot):
        for row in range(0, step[1], 32):
            tiles[slot][row : row + 32, :] = matern(dists[slot][row : row + 32, :])

    count = len(steps)
    for k in range(count + 2):
        if k >= 2:
            apply(steps[k - 2], tiles[k % 2])
        if 1 <= k <= count:
            fill(steps[k - 1], (k - 1) % 2)
        if k < count:
            measure(steps[k], dists[k % 2])


def pair_kernel(feats, names, *refs):
    ref = dict(zip(names, refs))
    rows_ref, cols_ref, right, out, back = (ref[name] for name in ("rows", "cols", "right", "out", "back"))
    count = rows_ref.shape[1]
    left = ref["left"]
    if "next_left" in ref:
        ref["next_left"][...] = left_side(cols_ref[:feats, :])
    put_right(right, cols_ref[:feats, :])
    out[...] = ref["acc"][...]
    back[...] = ref["back_acc"][...] if "back_acc" in ref else jnp.zeros_like(back)

    def measure(step, dist):
        row, rows, col = step
        dist[...] = dot(left[row : row + rows, :], right[:, col : col + COLS], ((1,), (0,)))

    def apply(step, tile):
        row, rows, col = step
        back[:, col : col + COLS] += dot(rows_ref[feats:, row : row + rows], tile[...], ((1,), (0,)))
        out[:, row : row + rows] += dot(cols_ref[feats:, col : col + COLS], tile[...], ((1,), (1,)))

    steps = [(row, ROWS, col) for col in range(0, count, COLS) for row in range(0, count, ROWS)]
    run_steps(steps, measure, apply, (ref["dist0"], ref["dist1"]), (ref["tile0"], ref["tile1"]))
    ref["out_ref"][...] = out[...].astype(ref["out_ref"].dtype)
    ref["back_ref"][...] = back[...].astype(ref["back_ref"].dtype)


def stage_buffers():
    return [
        pltpu.VMEM((ROWS, COLS), jnp.float32),
        pltpu.VMEM((ROWS, COLS), jnp.float32),
        pltpu.VMEM((ROWS, COLS), jnp.bfloat16),
        pltpu.VMEM((ROWS, COLS), jnp.bfloat16),
    ]


def pair(left, rows, cols, acc, feats, back_acc=None, out_dtype=jnp.float32, back_dtype=jnp.float32, next_left=False):
    probes, count = acc.shape
    given = {"left": left, "rows": rows, "cols": cols, "acc": acc}
    if back_acc is not None:
        given["back_acc"] = back_acc
    results = {
        "out_ref": jax.ShapeDtypeStruct((probes, count), out_dtype),
        "back_ref": jax.ShapeDtypeStruct((probes, count), back_dtype),
    }
    if next_left:
        results["next_left"] = jax.ShapeDtypeStruct(left.shape, left.dtype)
    made = {
        "right": pltpu.VMEM((DEPTH, count), jnp.bfloat16),
        "out": pltpu.VMEM((probes, count), jnp.float32),
        "back": pltpu.VMEM((probes, count), jnp.float32),
    }
    names = [*given, *results, *made, "dist0", "dist1", "tile0", "tile1"]
    return pl.pallas_call(
        functools.partial(pair_kernel, feats, names),
        out_shape=tuple(results.values()),
        in_specs=[VMEM] * len(given),
        out_specs=(VMEM,) * len(results),
        scratch_shapes=[*made.values(), *stage_buffers()],
        compiler_params=PARAMS,
        cost_estimate=COST,
        name="pair_tile",
    )(*given.values())


def self_steps(cols):
    steps = []
    for col in cols:
        row = 0
        while row < col + COLS:
            rows = min(ROWS, col + COLS - row)
            steps.append((row, rows, col))
            row += rows
    return steps


def run_self(cols, feats, left_ref, own_ref, out_ref, right, dists, tiles):
    def measure(step, dist):
        row, rows, col = step
        dist[:rows, :] = dot(left_ref[row : row + rows, :], right[:, col : col + COLS], ((1,), (0,)))

    def apply(step, tile):
        row, rows, col = step
        out_ref[:, col : col + COLS] += dot(own_ref[feats:, row : row + rows], tile[:rows, :], ((1,), (0,)))
        above = min(rows, col - row)
        if above:
            out_ref[:, row : row + above] += dot(own_ref[feats:, col : col + COLS], tile[:above, :], ((1,), (1,)))

    run_steps(self_steps(cols), measure, apply, dists, tiles)


def first_kernel(cols, feats, noise_ref, wide_ref, own_ref, left_ref, out_ref, copy_ref, right, dist0, dist1, tile0, tile1):
    left_ref[...] = left_side(own_ref[:feats, :])
    put_right(right, own_ref[:feats, :])
    out_ref[...] = wide_ref[...] * (noise_ref[0] * (1.0 / 3.0))
    copy_ref[...] = own_ref[...]
    run_self(cols, feats, left_ref, own_ref, out_ref, right, (dist0, dist1), (tile0, tile1))


def first_self(noise, wide, own, feats, cols):
    count = own.shape[1]
    probes = own.shape[0] - feats
    return pl.pallas_call(
        functools.partial(first_kernel, cols, feats),
        out_shape=(
            jax.ShapeDtypeStruct((count, DEPTH), jnp.bfloat16),
            jax.ShapeDtypeStruct((probes, count), jnp.float32),
            jax.ShapeDtypeStruct(own.shape, own.dtype),
        ),
        in_specs=[pl.BlockSpec(memory_space=pltpu.SMEM), VMEM, VMEM],
        out_specs=[VMEM] * 3,
        scratch_shapes=[pltpu.VMEM((DEPTH, count), jnp.bfloat16), *stage_buffers()],
        compiler_params=PARAMS,
        cost_estimate=COST,
        name="first_self",
    )(noise, wide, own)


def last_kernel(cols, feats, left_ref, own_ref, acc_ref, more_ref, out_ref, right, dist0, dist1, tile0, tile1):
    put_right(right, own_ref[:feats, :])
    out_ref[...] = acc_ref[...] + more_ref[...].astype(jnp.float32)
    run_self(cols, feats, left_ref, own_ref, out_ref, right, (dist0, dist1), (tile0, tile1))


def last_self(left, own, acc, more, feats, cols):
    count = own.shape[1]
    return pl.pallas_call(
        functools.partial(last_kernel, cols, feats),
        out_shape=jax.ShapeDtypeStruct(acc.shape, jnp.float32),
        in_specs=[VMEM] * 4,
        out_specs=VMEM,
        scratch_shapes=[pltpu.VMEM((DEPTH, count), jnp.bfloat16), *stage_buffers()],
        compiler_params=PARAMS,
        cost_estimate=COST,
        name="last_self",
    )(left, own, acc, more)


def move(shard, by):
    count = lax.axis_size("grp") * lax.axis_size("dev")
    return lax.ppermute(shard, ("grp", "dev"), [(i, (i + by) % count) for i in range(count)])


def gather(partial, axis):
    size = lax.axis_size(axis)
    return lax.all_to_all(jnp.broadcast_to(partial[None, :], (size, partial.shape[0])), axis, 0, 0)


def finish_kernel(count, parts_ref, product_ref, out_ref, curvature_ref):
    probes = product_ref.shape[0]
    mean = jnp.sum(parts_ref[...], axis=0, keepdims=True) * (1.0 / count)
    curvature_ref[...] = mean[:, :probes]
    scale = lax.rsqrt(mean[:, probes:] + 1e-06)
    row = lax.broadcasted_iota(jnp.int32, (probes, probes), 0)
    col = lax.broadcasted_iota(jnp.int32, (probes, probes), 1)
    scale = jnp.sum(jnp.where(row == col, scale, 0.0), axis=1, keepdims=True)
    out_ref[...] = product_ref[...] * scale


def finish(parts, product, count):
    return pl.pallas_call(
        functools.partial(finish_kernel, count),
        out_shape=(
            jax.ShapeDtypeStruct(product.shape, jnp.float32),
            jax.ShapeDtypeStruct((1, product.shape[0]), jnp.float32),
        ),
        compiler_params=PARAMS,
        cost_estimate=COST,
        name="finish",
    )(parts, product)


def per_device(points, inv_scale, probes, noise):
    feats = points.shape[1]
    wide = probes.T
    scaled = (points.T.astype(jnp.float32) * inv_scale[:, None]).astype(jnp.bfloat16)
    rounded = wide.astype(jnp.bfloat16)
    own = jnp.concatenate([scaled, rounded], axis=0)
    width = lax.axis_size("dev")
    wide_far = move(own, -width)
    columns = list(range(0, points.shape[0], COLS))
    late = len(columns) // 4
    left, acc, again = first_self(noise, wide, own, feats, columns[:-late])
    near = move(again, 1)
    acc, far_acc, far_left = pair(left, own, wide_far, acc, feats, next_left=True)
    to_far, near_acc = pair(far_left, wide_far, near, far_acc, feats, out_dtype=jnp.bfloat16)
    from_far = move(to_far, width)
    acc, to_near = pair(left, own, near, acc, feats, back_acc=near_acc, back_dtype=jnp.bfloat16)
    from_near = move(to_near, -1)
    acc = last_self(left, own, acc, from_far, feats, columns[-late:])
    product = (acc + from_near.astype(jnp.float32)) * 3.0
    count = lax.axis_size("grp") * width * probes.shape[0]
    sums = jnp.concatenate(
        [jnp.sum(rounded.astype(jnp.float32) * product, axis=1), jnp.sum(product * product, axis=1)]
    )
    sums = jnp.sum(gather(sums, "dev"), axis=0)
    normalized, curvature = finish(gather(sums, "grp"), product, count)
    return (normalized.T, curvature[0])


def solution(mesh):
    placed = (P(("grp", "dev"), None), P(), P(("grp", "dev"), None), P())
    return jax.shard_map(
        per_device,
        mesh=mesh,
        in_specs=placed,
        out_specs=(P(("grp", "dev"), None), P()),
        check_vma=False,
    )
```

```python
import functools

import jax
import jax.numpy as jnp
from jax import lax
from jax.experimental import pallas as pl
from jax.experimental.pallas import tpu as pltpu
from jax.sharding import PartitionSpec as P

LOG2E = 1.4426950408889634
DEPTH = 256
EXTRA = 16
COLS = 256
ROWS = 512
VMEM = pl.BlockSpec(memory_space=pltpu.VMEM)
COST = pl.CostEstimate(flops=1000, bytes_accessed=1000, transcendentals=0)
PARAMS = pltpu.CompilerParams(vmem_limit_bytes=32 * 2**20)


def dot(left, right, dims):
    return lax.dot_general(left, right, (dims, ((), ())), preferred_element_type=jnp.float32)


def matern(third_sq):
    third_sq = jnp.maximum(third_sq, 1e-30)
    third = third_sq * lax.rsqrt(third_sq)
    decay = jnp.exp2(third * (-3.0 * LOG2E))
    return ((third_sq + (third + 1.0 / 3.0)) * decay).astype(jnp.bfloat16)


def split3(wide):
    high = wide.astype(jnp.bfloat16)
    rest = wide - high.astype(jnp.float32)
    mid = rest.astype(jnp.bfloat16)
    low = (rest - mid.astype(jnp.float32)).astype(jnp.bfloat16)
    return high, mid, low


def extra_rows(features, left):
    wide = features.astype(jnp.float32)
    parts = split3(jnp.sum(wide * wide, axis=0, keepdims=True) * (5.0 / 9.0))
    row = lax.broadcasted_iota(jnp.int32, (EXTRA, features.shape[1]), 0)
    first, ones = (3, 0) if left else (0, 3)
    extra = jnp.where((row >= ones) & (row < ones + 3), 1.0, 0.0)
    for k, part in enumerate(parts):
        extra = jnp.where(row == first + k, part.astype(jnp.float32), extra)
    return extra.astype(jnp.bfloat16)


def left_side(features):
    feats, count = features.shape
    parts = split3(features.astype(jnp.float32) * (-10.0 / 9.0))
    rest = jnp.zeros((DEPTH - 3 * feats - EXTRA, count), jnp.bfloat16)
    return jnp.concatenate([*parts, extra_rows(features, True), rest], axis=0).T


def put_right(right, features):
    feats, count = features.shape
    for k in range(3):
        right[k * feats : (k + 1) * feats, :] = features
    right[3 * feats : 3 * feats + EXTRA, :] = extra_rows(features, False)
    right[3 * feats + EXTRA :, :] = jnp.zeros((DEPTH - 3 * feats - EXTRA, count), jnp.bfloat16)


def run_steps(steps, measure, apply, dists, tiles):
    def fill(step, slot):
        for row in range(0, step[1], 32):
            tiles[slot][row : row + 32, :] = matern(dists[slot][row : row + 32, :])

    count = len(steps)
    for k in range(count + 2):
        if k >= 2:
            apply(steps[k - 2], tiles[k % 2])
        if 1 <= k <= count:
            fill(steps[k - 1], (k - 1) % 2)
        if k < count:
            measure(steps[k], dists[k % 2])


def pair_kernel(feats, names, *refs):
    ref = dict(zip(names, refs))
    rows_ref, cols_ref, right, out, back = (ref[name] for name in ("rows", "cols", "right", "out", "back"))
    count = rows_ref.shape[1]
    left = ref["left"]
    if "next_left" in ref:
        ref["next_left"][...] = left_side(cols_ref[:feats, :])
    put_right(right, cols_ref[:feats, :])
    out[...] = ref["acc"][...]
    back[...] = ref["back_acc"][...] if "back_acc" in ref else jnp.zeros_like(back)

    def measure(step, dist):
        row, rows, col = step
        dist[...] = dot(left[row : row + rows, :], right[:, col : col + COLS], ((1,), (0,)))

    def apply(step, tile):
        row, rows, col = step
        back[:, col : col + COLS] += dot(rows_ref[feats:, row : row + rows], tile[...], ((1,), (0,)))
        out[:, row : row + rows] += dot(cols_ref[feats:, col : col + COLS], tile[...], ((1,), (1,)))

    steps = [(row, ROWS, col) for col in range(0, count, COLS) for row in range(0, count, ROWS)]
    run_steps(steps, measure, apply, (ref["dist0"], ref["dist1"]), (ref["tile0"], ref["tile1"]))
    ref["out_ref"][...] = out[...].astype(ref["out_ref"].dtype)
    ref["back_ref"][...] = back[...].astype(ref["back_ref"].dtype)


def stage_buffers():
    return [
        pltpu.VMEM((ROWS, COLS), jnp.float32),
        pltpu.VMEM((ROWS, COLS), jnp.float32),
        pltpu.VMEM((ROWS, COLS), jnp.bfloat16),
        pltpu.VMEM((ROWS, COLS), jnp.bfloat16),
    ]


def pair(left, rows, cols, acc, feats, back_acc=None, out_dtype=jnp.float32, back_dtype=jnp.float32, next_left=False):
    probes, count = acc.shape
    given = {"left": left, "rows": rows, "cols": cols, "acc": acc}
    if back_acc is not None:
        given["back_acc"] = back_acc
    results = {
        "out_ref": jax.ShapeDtypeStruct((probes, count), out_dtype),
        "back_ref": jax.ShapeDtypeStruct((probes, count), back_dtype),
    }
    if next_left:
        results["next_left"] = jax.ShapeDtypeStruct(left.shape, left.dtype)
    made = {
        "right": pltpu.VMEM((DEPTH, count), jnp.bfloat16),
        "out": pltpu.VMEM((probes, count), jnp.float32),
        "back": pltpu.VMEM((probes, count), jnp.float32),
    }
    names = [*given, *results, *made, "dist0", "dist1", "tile0", "tile1"]
    return pl.pallas_call(
        functools.partial(pair_kernel, feats, names),
        out_shape=tuple(results.values()),
        in_specs=[VMEM] * len(given),
        out_specs=(VMEM,) * len(results),
        scratch_shapes=[*made.values(), *stage_buffers()],
        compiler_params=PARAMS,
        cost_estimate=COST,
        name="pair_tile",
    )(*given.values())


def self_steps(cols):
    steps = []
    for col in cols:
        row = 0
        while row < col + COLS:
            rows = min(ROWS, col + COLS - row)
            steps.append((row, rows, col))
            row += rows
    return steps


def run_self(cols, feats, left_ref, own_ref, out_ref, right, dists, tiles):
    def measure(step, dist):
        row, rows, col = step
        dist[:rows, :] = dot(left_ref[row : row + rows, :], right[:, col : col + COLS], ((1,), (0,)))

    def apply(step, tile):
        row, rows, col = step
        out_ref[:, col : col + COLS] += dot(own_ref[feats:, row : row + rows], tile[:rows, :], ((1,), (0,)))
        above = min(rows, col - row)
        if above:
            out_ref[:, row : row + above] += dot(own_ref[feats:, col : col + COLS], tile[:above, :], ((1,), (1,)))

    run_steps(self_steps(cols), measure, apply, dists, tiles)


def first_kernel(cols, feats, noise_ref, wide_ref, own_ref, left_ref, out_ref, copy_ref, right, dist0, dist1, tile0, tile1):
    left_ref[...] = left_side(own_ref[:feats, :])
    put_right(right, own_ref[:feats, :])
    out_ref[...] = wide_ref[...] * (noise_ref[0] * (1.0 / 3.0))
    copy_ref[...] = own_ref[...]
    run_self(cols, feats, left_ref, own_ref, out_ref, right, (dist0, dist1), (tile0, tile1))


def first_self(noise, wide, own, feats, cols):
    count = own.shape[1]
    probes = own.shape[0] - feats
    return pl.pallas_call(
        functools.partial(first_kernel, cols, feats),
        out_shape=(
            jax.ShapeDtypeStruct((count, DEPTH), jnp.bfloat16),
            jax.ShapeDtypeStruct((probes, count), jnp.float32),
            jax.ShapeDtypeStruct(own.shape, own.dtype),
        ),
        in_specs=[pl.BlockSpec(memory_space=pltpu.SMEM), VMEM, VMEM],
        out_specs=[VMEM] * 3,
        scratch_shapes=[pltpu.VMEM((DEPTH, count), jnp.bfloat16), *stage_buffers()],
        compiler_params=PARAMS,
        cost_estimate=COST,
        name="first_self",
    )(noise, wide, own)


def last_kernel(cols, feats, left_ref, own_ref, acc_ref, more_ref, out_ref, right, dist0, dist1, tile0, tile1):
    put_right(right, own_ref[:feats, :])
    out_ref[...] = acc_ref[...] + more_ref[...].astype(jnp.float32)
    run_self(cols, feats, left_ref, own_ref, out_ref, right, (dist0, dist1), (tile0, tile1))


def last_self(left, own, acc, more, feats, cols):
    count = own.shape[1]
    return pl.pallas_call(
        functools.partial(last_kernel, cols, feats),
        out_shape=jax.ShapeDtypeStruct(acc.shape, jnp.float32),
        in_specs=[VMEM] * 4,
        out_specs=VMEM,
        scratch_shapes=[pltpu.VMEM((DEPTH, count), jnp.bfloat16), *stage_buffers()],
        compiler_params=PARAMS,
        cost_estimate=COST,
        name="last_self",
    )(left, own, acc, more)


def move(shard, by):
    count = lax.axis_size("grp") * lax.axis_size("dev")
    return lax.ppermute(shard, ("grp", "dev"), [(i, (i + by) % count) for i in range(count)])


def gather(partial, axis):
    size = lax.axis_size(axis)
    return lax.all_to_all(jnp.broadcast_to(partial[None, :], (size, partial.shape[0])), axis, 0, 0)


def finish_kernel(count, parts_ref, product_ref, out_ref, curvature_ref):
    probes = product_ref.shape[0]
    mean = jnp.sum(parts_ref[...], axis=0, keepdims=True) * (1.0 / count)
    curvature_ref[...] = mean[:, :probes]
    scale = lax.rsqrt(mean[:, probes:] + 1e-06)
    row = lax.broadcasted_iota(jnp.int32, (probes, probes), 0)
    col = lax.broadcasted_iota(jnp.int32, (probes, probes), 1)
    scale = jnp.sum(jnp.where(row == col, scale, 0.0), axis=1, keepdims=True)
    out_ref[...] = product_ref[...] * scale


def finish(parts, product, count):
    return pl.pallas_call(
        functools.partial(finish_kernel, count),
        out_shape=(
            jax.ShapeDtypeStruct(product.shape, jnp.float32),
            jax.ShapeDtypeStruct((1, product.shape[0]), jnp.float32),
        ),
        compiler_params=PARAMS,
        cost_estimate=COST,
        name="finish",
    )(parts, product)


def per_device(points, inv_scale, probes, noise):
    feats = points.shape[1]
    wide = probes.T
    scaled = (points.T.astype(jnp.float32) * inv_scale[:, None]).astype(jnp.bfloat16)
    rounded = wide.astype(jnp.bfloat16)
    own = jnp.concatenate([scaled, rounded], axis=0)
    width = lax.axis_size("dev")
    wide_far = move(own, -width)
    columns = list(range(0, points.shape[0], COLS))
    late = len(columns) // 8
    left, acc, again = first_self(noise, wide, own, feats, columns[:-late])
    near = move(again, 1)
    acc, far_acc, far_left = pair(left, own, wide_far, acc, feats, next_left=True)
    to_far, near_acc = pair(far_left, wide_far, near, far_acc, feats, out_dtype=jnp.bfloat16)
    from_far = move(to_far, width)
    acc, to_near = pair(left, own, near, acc, feats, back_acc=near_acc, back_dtype=jnp.bfloat16)
    from_near = move(to_near, -1)
    acc = last_self(left, own, acc, from_far, feats, columns[-late:])
    product = (acc + from_near.astype(jnp.float32)) * 3.0
    count = lax.axis_size("grp") * width * probes.shape[0]
    sums = jnp.concatenate(
        [jnp.sum(rounded.astype(jnp.float32) * product, axis=1), jnp.sum(product * product, axis=1)]
    )
    sums = jnp.sum(gather(sums, "dev"), axis=0)
    normalized, curvature = finish(gather(sums, "grp"), product, count)
    return (normalized.T, curvature[0])


def solution(mesh):
    placed = (P(("grp", "dev"), None), P(), P(("grp", "dev"), None), P())
    return jax.shard_map(
        per_device,
        mesh=mesh,
        in_specs=placed,
        out_specs=(P(("grp", "dev"), None), P()),
        check_vma=False,
    )
```
